32 devices in a mesh: row: 8 (over z, x), layer: 4 (over y, core).
Axes of the slice: x: 2, y: 2, z: 4, core: 2. Of those that a mesh axis runs over, the one named last changes fastest.
Arguments:
- left_factor: float32 [4096, 512], P('row'), may hold values from -6 to 6
- right_factor: float32 [4096, 512], P(('row', 'layer')), may hold values from -0.25 to 0.25
- block_columns: int32 [32, 8], P('row', 'layer'), may hold values from -1 to 31, as said below
- labels: int32 [32, 8, 128, 128], P('row', 'layer'), may hold values 0 or 1
Outputs:
- left_grad: float32 [4096, 512], P('row', 'layer')
The draws below stay inside these ranges and needn't reach their ends.
Inputs may be any that keep to these rules, and one draw needn't show every extreme that they name: `block_columns`: entries l*2 to (l+1)*2 - 1 of row t list, in ascending order and each once, occupied tile columns j of tile row t with j % 4 == l, then -1 in the unused slots; every list holds at least one column, and in every draw some list of each group l is full.
All inputs are finite; a program needn't handle non-finite values. No bound on the sum of `labels` on one device may be relied on, other than what follows from the above.
Results may differ from the reference program's by a relative error of at most 0.0003.
Values sent between devices are 32-bit elements; how exact they have to be, the bound alone decides.
A program may use at most 64 MiB of HBM per device.

```python
import jax
import jax.numpy as jnp
from jax import lax

K = 512
TILE = 128
SLOTS = 2
LAYERS = 4
ROWS = 4096
TROWS = 32
TCOLS = 32
NCOLS = 4096


def draw_block_columns(key, part):
    key_count, key_order, key_full = jax.random.split(key, 3)
    holders = TCOLS // LAYERS
    level = jax.random.randint(key_count, (TROWS, LAYERS), 1, SLOTS + 1)
    chosen = jax.random.randint(key_full, (LAYERS,), 0, TROWS)
    forced = lax.broadcasted_iota(jnp.int32, (TROWS, LAYERS), 0) == chosen[None, :]
    level = jnp.where(forced, SLOTS, level)
    counts = jnp.maximum(1, (level * level + level * SLOTS) // (2 * SLOTS))
    noise = jax.random.randint(key_order, (TROWS, LAYERS, holders), 0, 1 << 20)
    scores = noise * holders + lax.broadcasted_iota(jnp.int32, (TROWS, LAYERS, holders), 2)
    order = jnp.argsort(scores, axis=2, stable=True)[:, :, :SLOTS]
    order = jnp.sort(order, axis=2).astype(jnp.int32)
    slot_index = lax.broadcasted_iota(jnp.int32, (TROWS, LAYERS, SLOTS), 2)
    layer_index = lax.broadcasted_iota(jnp.int32, (TROWS, LAYERS, SLOTS), 1)
    columns = jnp.where(slot_index < counts[:, :, None], order * LAYERS + layer_index, -1)
    return columns.reshape(TROWS, LAYERS * SLOTS).astype(jnp.int32)


def set_ends(values, key, least, high):
    place = [jax.random.randint(jax.random.fold_in(key, axis), (), 0, length) for axis, length in enumerate(values.shape)]
    widest = values.shape.index(max(values.shape))
    next_to = place[:widest] + [(place[widest] + 1) % values.shape[widest]] + place[widest + 1:]
    return values.at[tuple(place)].set(least).at[tuple(next_to)].set(high)


def block_scale(own_key, dims, shards, low, high):
    def one(position, parts):
        draws = jax.random.uniform(jax.random.fold_in(jax.random.fold_in(own_key, 6), position), (parts,), jnp.float32, low / len(shards), high / len(shards))
        return jnp.repeat(jnp.exp(draws), dims[position] // parts).reshape((-1,) + (1,) * (len(dims) - position - 1))

    factor_of = one(*shards[0])
    for cut in shards[1:]:
        factor_of = factor_of * one(*cut)
    return factor_of


def bell_draw(own_key, dims, width, limit, cuts=(), dtype=jnp.bfloat16):
    values = jax.random.normal(own_key, dims, jnp.float32) * width
    if len(cuts) > 0:
        values = block_scale(own_key, dims, cuts, -0.22, 0.18) * values
    return jnp.clip(values, min=-limit, max=limit).astype(dtype)


def setup_inputs(seed: int = 0) -> dict:
    splits = jax.random.split(jax.random.key(seed), 5)
    left_factor = bell_draw(splits[0], (ROWS, K), 1.0, 6.0, ((0, 8),), jnp.float32)
    right_factor = bell_draw(splits[1], (NCOLS, K), K ** -0.5, 0.25, ((0, 32),), jnp.float32)
    block_columns = draw_block_columns(jax.random.fold_in(splits[4], 71), 0)
    labels = set_ends((jax.random.randint(splits[3], (TROWS, LAYERS * SLOTS, TILE, TILE), 0, 2) < 1).astype(jnp.int32), jax.random.fold_in(splits[3], 1), 0, 1)
    return {"left_factor": left_factor, "right_factor": right_factor, "block_columns": block_columns, "labels": labels}


shrink_rate = 0.1


def reference(left_factor, right_factor, block_columns, labels):
    right_tiles = right_factor.reshape(TCOLS, TILE, K)

    def one_row(inputs):
        left_rows, columns, targets = inputs
        occupied = (columns >= 0).astype(jnp.float32)
        picked = right_tiles[jnp.clip(columns, 0, TCOLS - 1).astype(jnp.int32)]
        scores = jnp.einsum("ak,sbk->sab", left_rows, picked, precision=lax.Precision.HIGHEST)
        residue = (jax.nn.sigmoid(scores) - targets.astype(jnp.float32)) * occupied[:, None, None]
        return jnp.einsum("sab,sbk->ak", residue, picked, precision=lax.Precision.HIGHEST)

    gradient = lax.map(one_row, (left_factor.reshape(TROWS, TILE, K), block_columns, labels))
    return gradient.reshape(ROWS, K) + shrink_rate * left_factor
```

```python
import functools

import jax
import jax.numpy as jnp
from jax import lax
from jax.experimental import pallas as pl
from jax.experimental.pallas import tpu as pltpu
from jax.sharding import PartitionSpec as P

shrink_rate = 0.1
MESH = pl.DeviceIdType.MESH
F32 = jnp.float32
BF16 = jnp.bfloat16


def place_of(index, count):
    odd = index % 2
    return (1 - odd) * (index // 2) + odd * (count - 1 - index // 2)


def index_at(place, count):
    back = place // (count // 2)
    return (1 - back) * (2 * place) + back * (2 * (count - 1 - place) + 1)


def loop(low, high, body):
    if high - low <= 4:
        for step in range(low, high):
            body(step)
    else:

        @pl.loop(low, high)
        def _(step):
            body(step)


def split(value):
    high = value.astype(BF16)
    return high, (value - high.astype(F32)).astype(BF16)


def product(a_pair, b_pair, dims):
    dot = functools.partial(
        lax.dot_general, dimension_numbers=(dims, ((), ())), preferred_element_type=F32
    )
    return dot(a_pair[0], b_pair[0]) + (dot(a_pair[0], b_pair[1]) + dot(a_pair[1], b_pair[0]))


def kernel(
    count, layers, left_hbm, right_hbm, columns, labels_hbm, out,
    tiles, left, left_high, left_low, labels, total, from_core, to_side, from_side,
    local_sem, ring_send, ring_recv, core_send, core_recv, side_send, side_recv,
):
    row, layer = lax.axis_index("row"), lax.axis_index("layer")
    half = count // 2
    size, width = tiles.shape[1], tiles.shape[2]
    trows, slots = labels.shape[0], labels.shape[1]
    part = width // layers
    chunk = size // 2
    sides = layers // 2
    place = place_of(row, count)
    ahead = index_at((place + 1) % count, count)
    behind = index_at((place + count - 1) % count, count)
    core = layer % 2
    side = layer // 2
    twin = side * 2 + (1 - core)
    side_layer = [((side + d) % sides) * 2 + core for d in range(sides)]

    barrier = pltpu.get_barrier_semaphore()
    partners = [(ahead, layer), (behind, layer), (row, twin)]
    partners += [(row, side_layer[d]) for d in range(1, sides)]
    for partner in partners:
        pl.semaphore_signal(barrier, inc=1, device_id=partner, device_id_type=MESH)

    copies = [
        pltpu.make_async_copy(right_hbm, tiles.at[0], local_sem.at[0]),
        pltpu.make_async_copy(left_hbm, left, local_sem.at[1]),
        pltpu.make_async_copy(labels_hbm, labels, local_sem.at[2]),
    ]
    for copy in copies:
        copy.start()
    copies[0].wait()
    pl.semaphore_wait(barrier, len(partners))

    def hop(direction, step, piece):
        if direction == 0:
            source, target, device = step, step + 1, ahead
        else:
            source, target, device = (count - step) % count, count - step - 1, behind
        rows = pl.ds(piece * chunk, chunk)
        return pltpu.make_async_remote_copy(
            src_ref=tiles.at[source, rows],
            dst_ref=tiles.at[target, rows],
            send_sem=ring_send.at[direction, step, piece],
            recv_sem=ring_recv.at[direction, step, piece],
            device_id=(device, layer),
            device_id_type=MESH,
        )

    every = [(0, 0), (1, 1), (0, 1), (1, 0)]

    def moves(last):
        return every[:2] if last else every

    def send(step, chosen):
        for direction, piece in chosen:
            hop(direction, step, piece).start()

    def holder(slot):
        return index_at((place + count - slot) % count, count) * layers + layer

    def residue_of(scores, slot, t):
        tile = holder(slot)
        listed = jnp.zeros((), F32)
        target = jnp.zeros((size, size), F32)
        for s in range(slots):
            match = (columns[t, s] == tile).astype(F32)
            listed = listed + match
            target = target + match * labels[t, s].astype(F32)
        return jax.nn.sigmoid(scores) * listed - target

    def add_tiles(chosen, first):
        value = jnp.concatenate([tiles[slot] for slot in chosen], axis=0)
        right_pair = split(value)
        scores = product((left_high[...], left_low[...]), right_pair, ((1,), (1,)))
        residue = jnp.concatenate(
            [
                jnp.concatenate(
                    [
                        residue_of(
                            scores[t * size:(t + 1) * size, i * size:(i + 1) * size], slot, t
                        )
                        for i, slot in enumerate(chosen)
                    ],
                    axis=1,
                )
                for t in range(trows)
            ],
            axis=0,
        )
        term = product(split(residue), right_pair, ((1,), (0,)))
        for m in range(layers):
            columns_of = term[:, m * part:(m + 1) * part]
            total[m] = columns_of if first else total[m] + columns_of

    send(0, moves(half == 1))
    copies[1].wait()
    high, low = split(left[...])
    left_high[...] = high
    left_low[...] = low
    copies[2].wait()
    add_tiles([0], True)

    def middle(step, last):
        order = moves(last)
        for direction, piece in every:
            hop(direction, step - 1, piece).wait_recv()
            if (direction, piece) in order:
                hop(direction, step, piece).start()
        add_tiles([step, count - step], False)

    loop(1, half - 1, lambda step: middle(step, False))
    if half > 1:
        middle(half - 1, True)
    for direction, piece in moves(True):
        hop(direction, half - 1, piece).wait_recv()
    add_tiles([half], False)

    def core_copy(d):
        return pltpu.make_async_remote_copy(
            src_ref=total.at[((side + d) % sides) * 2 + (1 - core)],
            dst_ref=from_core.at[d],
            send_sem=core_send.at[d],
            recv_sem=core_recv.at[d],
            device_id=(row, twin),
            device_id_type=MESH,
        )

    def side_copy(d):
        return pltpu.make_async_remote_copy(
            src_ref=to_side.at[d - 1],
            dst_ref=from_side.at[d - 1],
            send_sem=side_send.at[d - 1],
            recv_sem=side_recv.at[d - 1],
            device_id=(row, side_layer[d]),
            device_id_type=MESH,
        )

    away = list(range(1, sides)) + [0]
    for d in away:
        core_copy(d).start()
    for d in away:
        core_copy(d).wait_recv()
        own = total[side_layer[d]] + from_core[d]
        if d:
            to_side[d - 1] = own
            side_copy(d).start()
        else:
            out[...] = own + shrink_rate * left[:, pl.ds(pl.multiple_of(layer * part, part), part)]
    for d in range(1, sides):
        side_copy(d).wait_recv()
        out[...] += from_side[d - 1]

    for d in range(1, sides):
        side_copy(d).wait_send()
    for d in away:
        core_copy(d).wait_send()

    def drain(step):
        for direction, piece in every:
            hop(direction, step, piece).wait_send()

    loop(0, half - 1, drain)
    for direction, piece in moves(True):
        hop(direction, half - 1, piece).wait_send()


def per_device(left_factor, right_factor, block_columns, labels):
    count, layers = lax.axis_size("row"), lax.axis_size("layer")
    size, width = right_factor.shape
    rows = left_factor.shape[0]
    part, half, sides = width // layers, count // 2, layers // 2
    dma = pltpu.SemaphoreType.DMA
    return pl.pallas_call(
        functools.partial(kernel, count, layers),
        out_shape=jax.ShapeDtypeStruct((rows, part), F32),
        in_specs=[
            pl.BlockSpec(memory_space=pl.ANY),
            pl.BlockSpec(memory_space=pl.ANY),
            pl.BlockSpec(memory_space=pltpu.SMEM),
            pl.BlockSpec(memory_space=pl.ANY),
        ],
        out_specs=pl.BlockSpec(memory_space=pltpu.VMEM),
        scratch_shapes=[
            pltpu.VMEM((count, size, width), F32),
            pltpu.VMEM((rows, width), F32),
            pltpu.VMEM((rows, width), BF16),
            pltpu.VMEM((rows, width), BF16),
            pltpu.VMEM(labels.shape, jnp.int32),
            pltpu.VMEM((layers, rows, part), F32),
            pltpu.VMEM((sides, rows, part), F32),
            pltpu.VMEM((max(sides - 1, 1), rows, part), F32),
            pltpu.VMEM((max(sides - 1, 1), rows, part), F32),
            dma((3,)),
            dma((2, half, 2)),
            dma((2, half, 2)),
            dma((sides,)),
            dma((sides,)),
            dma((max(sides - 1, 1),)),
            dma((max(sides - 1, 1),)),
        ],
        compiler_params=pltpu.CompilerParams(
            collective_id=0, has_side_effects=True, vmem_limit_bytes=56 * 1024 * 1024
        ),
        cost_estimate=pl.CostEstimate(
            flops=12 * rows * width * size * count,
            bytes_accessed=4 * (rows * width + count * size * width + labels.size + rows * part),
            transcendentals=rows * size * count,
        ),
    )(left_factor, right_factor, block_columns, labels)


def solution(mesh):
    in_specs = (
        P("row", None),
        P(("row", "layer"), None),
        P("row", "layer"),
        P("row", "layer", None, None),
    )
    out_specs = P("row", "layer")
    return jax.shard_map(
        per_device, mesh=mesh, in_specs=in_specs, out_specs=out_specs, check_vma=False
    )
```

```python
import functools

import jax
import jax.numpy as jnp
from jax import lax
from jax.experimental import pallas as pl
from jax.experimental.pallas import tpu as pltpu
from jax.sharding import PartitionSpec as P

shrink_rate = 0.1
pieces = 2
stride = 1
MESH = pl.DeviceIdType.MESH
F32 = jnp.float32
BF16 = jnp.bfloat16


def place_of(index, count):
    odd = index % 2
    return (1 - odd) * (index // 2) + odd * (count - 1 - index // 2)


def index_at(place, count):
    back = place // (count // 2)
    return (1 - back) * (2 * place) + back * (2 * (count - 1 - place) + 1)


def loop(low, high, body):
    if high - low <= 4:
        for step in range(low, high):
            body(step)
    else:

        @pl.loop(low, high)
        def _(step):
            body(step)


def split(value):
    high = value.astype(BF16)
    return high, (value - high.astype(F32)).astype(BF16)


def product(a_pair, b_pair, dims):
    dot = functools.partial(
        lax.dot_general, dimension_numbers=(dims, ((), ())), preferred_element_type=F32
    )
    return dot(a_pair[0], b_pair[0]) + (dot(a_pair[0], b_pair[1]) + dot(a_pair[1], b_pair[0]))


def kernel(
    count, layers, left_hbm, right_hbm, columns, labels_hbm, out,
    tiles, left, left_high, left_low, labels, total, from_core, to_side, from_side,
    local_sem, ring_send, ring_recv, core_send, core_recv, side_send, side_recv,
):
    row, layer = lax.axis_index("row"), lax.axis_index("layer")
    half = count // 2
    size, width = tiles.shape[1], tiles.shape[2]
    trows, slots = labels.shape[0], labels.shape[1]
    part = width // layers
    chunk = size // pieces
    sides = layers // 2
    place = place_of(row, count)
    ahead = index_at((place + 1) % count, count)
    behind = index_at((place + count - 1) % count, count)
    core = layer % 2
    side = layer // 2
    twin = side * 2 + (1 - core)
    side_layer = [((side + d) % sides) * 2 + core for d in range(sides)]

    barrier = pltpu.get_barrier_semaphore()
    partners = [(ahead, layer), (behind, layer), (row, twin)]
    partners += [(row, side_layer[d]) for d in range(1, sides)]
    for partner in partners:
        pl.semaphore_signal(barrier, inc=1, device_id=partner, device_id_type=MESH)

    copies = [
        pltpu.make_async_copy(right_hbm, tiles.at[0], local_sem.at[0]),
        pltpu.make_async_copy(left_hbm, left, local_sem.at[1]),
        pltpu.make_async_copy(labels_hbm, labels, local_sem.at[2]),
    ]
    for copy in copies:
        copy.start()
    copies[0].wait()
    pl.semaphore_wait(barrier, len(partners))

    def hop(direction, step, piece):
        if direction == 0:
            source, target, device = step, step + 1, ahead
        else:
            source, target, device = (count - step) % count, count - step - 1, behind
        rows = pl.ds(piece * chunk, chunk)
        own = isinstance(step, int) and step == 0
        return pltpu.make_async_remote_copy(
            src_ref=tiles.at[source, rows],
            dst_ref=tiles.at[target, rows],
            send_sem=ring_send.at[direction, step, piece],
            recv_sem=ring_recv.at[direction, step, piece],
            device_id=(device, layer),
            device_id_type=MESH,
        )

    every = [(d, (pieces - 1 - i) if d else i) for i in range(pieces) for d in range(2)]

    def moves(last):
        return every[:pieces] if last else every

    def send(step, chosen):
        for direction, piece in chosen:
            hop(direction, step, piece).start()

    def holder(slot):
        return index_at((place + count - slot) % count, count) * layers + layer

    def residue_of(scores, slot, t):
        tile = holder(slot)
        listed = jnp.zeros((), F32)
        target = jnp.zeros((size, size), F32)
        for s in range(slots):
            match = (columns[s, t] == tile).astype(F32)
            listed = listed + match
            target = target + match * labels[t, s].astype(F32)
        return jax.nn.sigmoid(scores) * listed - target

    def pair_of(chosen):
        return split(jnp.concatenate([tiles[slot] for slot in chosen], axis=0))

    def add_tiles(chosen, right_pair, low, high, first=False):
        rows = slice(low * size, high * size)
        scores = product((left_high[rows], left_low[rows]), right_pair, ((1,), (1,)))
        residue = jnp.concatenate(
            [
                jnp.concatenate(
                    [
                        residue_of(
                            scores[(t - low) * size:(t - low + 1) * size, i * size:(i + 1) * size],
                            slot,
                            t,
                        )
                        for i, slot in enumerate(chosen)
                    ],
                    axis=1,
                )
                for t in range(low, high)
            ],
            axis=0,
        )
        term = product(split(residue), right_pair, ((1,), (0,)))
        for m in range(layers):
            columns_of = term[:, m * part:(m + 1) * part]
            total[m, rows] = columns_of if first else total[m, rows] + columns_of

    send(0, moves(half == 1))
    copies[1].wait()
    high, low = split(left[...])
    left_high[...] = high
    left_low[...] = low
    copies[2].wait()
    add_tiles([0], pair_of([0]), 0, trows, True)

    def middle(step, last):
        order = moves(last)
        for direction, piece in every:
            hop(direction, step - 1, piece).wait_recv()
            if (direction, piece) in order:
                hop(direction, step, piece).start()
        chosen = [step, count - step]
        add_tiles(chosen, pair_of(chosen), 0, trows)

    loop(1, half - 1, lambda step: middle(step, False))
    if half > 1:
        middle(half - 1, True)
    for direction, piece in moves(True):
        hop(direction, half - 1, piece).wait_recv()

    def group_rows(g):
        return pl.ds(g * size, size)

    def core_copy(d, g):
        return pltpu.make_async_remote_copy(
            src_ref=total.at[((side + d) % sides) * 2 + (1 - core), group_rows(g)],
            dst_ref=from_core.at[d, group_rows(g)],
            send_sem=core_send.at[d, g],
            recv_sem=core_recv.at[d, g],
            device_id=(row, twin),
            device_id_type=MESH,
        )

    def side_copy(d, g):
        return pltpu.make_async_remote_copy(
            src_ref=to_side.at[d - 1, group_rows(g)],
            dst_ref=from_side.at[d - 1, group_rows(g)],
            send_sem=side_send.at[d - 1, g],
            recv_sem=side_recv.at[d - 1, g],
            device_id=(row, side_layer[d]),
            device_id_type=MESH,
        )

    def pass_on(g):
        rows = group_rows(g)
        for d in range(1, sides):
            core_copy(d, g).wait_recv()
            to_side[d - 1, rows] = total[side_layer[d], rows] + from_core[d, rows]
            side_copy(d, g).start()

    last_pair = pair_of([half])
    for low in range(0, trows, stride):
        groups = range(low, min(low + stride, trows))
        add_tiles([half], last_pair, low, groups[-1] + 1)
        for d in range(1, sides):
            for g in groups:
                core_copy(d, g).start()
        if low:
            for g in range(low - stride, low):
                pass_on(g)
    for g in groups:
        pass_on(g)
    for g in range(trows):
        core_copy(0, g).start()
    own_part = pl.ds(pl.multiple_of(layer * part, part), part)
    for g in range(trows):
        rows = group_rows(g)
        core_copy(0, g).wait_recv()
        out[rows] = total[layer, rows] + from_core[0, rows] + shrink_rate * left[rows, own_part]
    for g in range(trows):
        rows = group_rows(g)
        for d in range(1, sides):
            side_copy(d, g).wait_recv()
            out[rows] += from_side[d - 1, rows]

    for g in range(trows):
        for d in range(1, sides):
            side_copy(d, g).wait_send()
        for d in range(sides):
            core_copy(d, g).wait_send()

    def drain(step):
        for direction, piece in every:
            hop(direction, step, piece).wait_send()

    if half > 1:
        drain(0)
    loop(1, half - 1, drain)
    for direction, piece in moves(True):
        hop(direction, half - 1, piece).wait_send()


def per_device(left_factor, right_factor, block_columns, labels):
    count, layers = lax.axis_size("row"), lax.axis_size("layer")
    size, width = right_factor.shape
    rows = left_factor.shape[0]
    trows = labels.shape[0]
    part, half, sides = width // layers, count // 2, layers // 2
    dma = pltpu.SemaphoreType.DMA
    return pl.pallas_call(
        functools.partial(kernel, count, layers),
        out_shape=pltpu.VMEM((rows, part), F32),
        in_specs=[
            pl.BlockSpec(memory_space=pl.ANY),
            pl.BlockSpec(memory_space=pl.ANY),
            pl.BlockSpec(memory_space=pltpu.SMEM),
            pl.BlockSpec(memory_space=pl.ANY),
        ],
        out_specs=pl.BlockSpec(memory_space=pltpu.VMEM),
        scratch_shapes=[
            pltpu.VMEM((count, size, width), F32),
            pltpu.VMEM((rows, width), F32),
            pltpu.VMEM((rows, width), BF16),
            pltpu.VMEM((rows, width), BF16),
            pltpu.VMEM(labels.shape, jnp.int32),
            pltpu.VMEM((layers, rows, part), F32),
            pltpu.VMEM((sides, rows, part), F32),
            pltpu.VMEM((max(sides - 1, 1), rows, part), F32),
            pltpu.VMEM((max(sides - 1, 1), rows, part), F32),
            dma((3,)),
            dma((2, half, pieces)),
            dma((2, half, pieces)),
            dma((sides, trows)),
            dma((sides, trows)),
            dma((max(sides - 1, 1), trows)),
            dma((max(sides - 1, 1), trows)),
        ],
        compiler_params=pltpu.CompilerParams(
            collective_id=0, has_side_effects=True, vmem_limit_bytes=56 * 1024 * 1024
        ),
        cost_estimate=pl.CostEstimate(
            flops=12 * rows * width * size * count,
            bytes_accessed=4 * (rows * width + count * size * width + labels.size + rows * part),
            transcendentals=rows * size * count,
        ),
    )(left_factor, right_factor, block_columns.T, labels)


def solution(mesh):
    in_specs = (
        P("row", None),
        P(("row", "layer"), None),
        P("row", "layer"),
        P("row", "layer", None, None),
    )
    out_specs = P("row", "layer")
    return jax.shard_map(
        per_device, mesh=mesh, in_specs=in_specs, out_specs=out_specs, check_vma=False
    )
```

```python
import functools

import jax
import jax.numpy as jnp
from jax import lax
from jax.experimental import pallas as pl
from jax.experimental.pallas import tpu as pltpu
from jax.sharding import PartitionSpec as P

shrink_rate = 0.1
pieces = 2
stride = 1
MESH = pl.DeviceIdType.MESH
F32 = jnp.float32
BF16 = jnp.bfloat16


def place_of(index, count):
    odd = index % 2
    return (1 - odd) * (index // 2) + odd * (count - 1 - index // 2)


def index_at(place, count):
    back = place // (count // 2)
    return (1 - back) * (2 * place) + back * (2 * (count - 1 - place) + 1)


def loop(low, high, body):
    if high - low <= 4:
        for step in range(low, high):
            body(step)
    else:

        @pl.loop(low, high)
        def _(step):
            body(step)


def split(value):
    high = value.astype(BF16)
    return high, (value - high.astype(F32)).astype(BF16)


def product(a_pair, b_pair, dims):
    dot = functools.partial(
        lax.dot_general, dimension_numbers=(dims, ((), ())), preferred_element_type=F32
    )
    return dot(a_pair[0], b_pair[0]) + (dot(a_pair[0], b_pair[1]) + dot(a_pair[1], b_pair[0]))


def kernel(
    count, layers, left_hbm, right_hbm, columns_hbm, labels_hbm, out,
    tiles, left, left_high, left_low, labels, columns, total, from_core, to_side, from_side,
    local_sem, ring_send, ring_recv, core_send, core_recv, side_send, side_recv,
):
    row, layer = lax.axis_index("row"), lax.axis_index("layer")
    half = count // 2
    size, width = tiles.shape[1], tiles.shape[2]
    trows, slots = labels.shape[0], labels.shape[1]
    part = width // layers
    chunk = size // pieces
    sides = layers // 2
    place = place_of(row, count)
    ahead = index_at((place + 1) % count, count)
    behind = index_at((place + count - 1) % count, count)
    core = layer % 2
    side = layer // 2
    twin = side * 2 + (1 - core)
    side_layer = [((side + d) % sides) * 2 + core for d in range(sides)]

    barrier = pltpu.get_barrier_semaphore()
    partners = [(ahead, layer), (behind, layer), (row, twin)]
    partners += [(row, side_layer[d]) for d in range(1, sides)]
    for partner in partners:
        pl.semaphore_signal(barrier, inc=1, device_id=partner, device_id_type=MESH)

    copies = [
        pltpu.make_async_copy(right_hbm, tiles.at[0], local_sem.at[0]),
        pltpu.make_async_copy(left_hbm, left, local_sem.at[1]),
        pltpu.make_async_copy(labels_hbm, labels, local_sem.at[2]),
        pltpu.make_async_copy(columns_hbm, columns, local_sem.at[3]),
    ]
    copies[0].start()
    copies[0].wait()
    pl.semaphore_wait(barrier, len(partners))

    def hop(direction, step, piece):
        if direction == 0:
            source, target, device = step, step + 1, ahead
        else:
            source, target, device = (count - step) % count, count - step - 1, behind
        rows = pl.ds(piece * chunk, chunk)
        own = isinstance(step, int) and step == 0
        return pltpu.make_async_remote_copy(
            src_ref=tiles.at[source, rows],
            dst_ref=tiles.at[target, rows],
            send_sem=ring_send.at[direction, step, piece],
            recv_sem=ring_recv.at[direction, step, piece],
            device_id=(device, layer),
            device_id_type=MESH,
        )

    every = [(d, (pieces - 1 - i) if d else i) for i in range(pieces) for d in range(2)]

    def moves(last):
        return every[:pieces] if last else every

    def send(step, chosen):
        for direction, piece in chosen:
            hop(direction, step, piece).start()

    def holder(slot):
        return index_at((place + count - slot) % count, count) * layers + layer

    def residue_of(scores, slot, t):
        tile = holder(slot)
        listed = jnp.zeros((), F32)
        target = jnp.zeros((size, size), F32)
        for s in range(slots):
            match = (columns[s, t] == tile).astype(F32)
            listed = listed + match
            target = target + match * labels[t, s].astype(F32)
        return jax.nn.sigmoid(scores) * listed - target

    def pair_of(chosen):
        return split(jnp.concatenate([tiles[slot] for slot in chosen], axis=0))

    def add_tiles(chosen, right_pair, low, high, first=False):
        rows = slice(low * size, high * size)
        scores = product((left_high[rows], left_low[rows]), right_pair, ((1,), (1,)))
        residue = jnp.concatenate(
            [
                jnp.concatenate(
                    [
                        residue_of(
                            scores[(t - low) * size:(t - low + 1) * size, i * size:(i + 1) * size],
                            slot,
                            t,
                        )
                        for i, slot in enumerate(chosen)
                    ],
                    axis=1,
                )
                for t in range(low, high)
            ],
            axis=0,
        )
        term = product(split(residue), right_pair, ((1,), (0,)))
        for m in range(layers):
            columns_of = term[:, m * part:(m + 1) * part]
            total[m, rows] = columns_of if first else total[m, rows] + columns_of

    send(0, moves(half == 1))
    for copy in copies[1:]:
        copy.start()
    copies[1].wait()
    high, low = split(left[...])
    left_high[...] = high
    left_low[...] = low
    copies[2].wait()
    copies[3].wait()
    add_tiles([0], pair_of([0]), 0, trows, True)

    def middle(step, last):
        order = moves(last)
        for direction, piece in every:
            hop(direction, step - 1, piece).wait_recv()
            if (direction, piece) in order:
                hop(direction, step, piece).start()
        chosen = [step, count - step]
        add_tiles(chosen, pair_of(chosen), 0, trows)

    loop(1, half - 1, lambda step: middle(step, False))
    if half > 1:
        middle(half - 1, True)
    for direction, piece in moves(True):
        hop(direction, half - 1, piece).wait_recv()

    def group_rows(g):
        return pl.ds(g * size, size)

    def core_copy(d, g):
        return pltpu.make_async_remote_copy(
            src_ref=total.at[((side + d) % sides) * 2 + (1 - core), group_rows(g)],
            dst_ref=from_core.at[d, group_rows(g)],
            send_sem=core_send.at[d, g],
            recv_sem=core_recv.at[d, g],
            device_id=(row, twin),
            device_id_type=MESH,
        )

    def side_copy(d, g):
        return pltpu.make_async_remote_copy(
            src_ref=to_side.at[d - 1, group_rows(g)],
            dst_ref=from_side.at[d - 1, group_rows(g)],
            send_sem=side_send.at[d - 1, g],
            recv_sem=side_recv.at[d - 1, g],
            device_id=(row, side_layer[d]),
            device_id_type=MESH,
        )

    def pass_on(g):
        rows = group_rows(g)
        for d in range(1, sides):
            core_copy(d, g).wait_recv()
            to_side[d - 1, rows] = total[side_layer[d], rows] + from_core[d, rows]
            side_copy(d, g).start()

    last_pair = pair_of([half])
    for low in range(0, trows, stride):
        groups = range(low, min(low + stride, trows))
        add_tiles([half], last_pair, low, groups[-1] + 1)
        for d in range(1, sides):
            for g in groups:
                core_copy(d, g).start()
        if low:
            for g in range(low - stride, low):
                pass_on(g)
    for g in groups:
        pass_on(g)
    for g in range(trows):
        core_copy(0, g).start()
    own_part = pl.ds(pl.multiple_of(layer * part, part), part)
    for g in range(trows):
        rows = group_rows(g)
        core_copy(0, g).wait_recv()
        out[rows] = total[layer, rows] + from_core[0, rows] + shrink_rate * left[rows, own_part]
    for g in range(trows):
        rows = group_rows(g)
        for d in range(1, sides):
            side_copy(d, g).wait_recv()
            out[rows] += from_side[d - 1, rows]

    for g in range(trows):
        for d in range(1, sides):
            side_copy(d, g).wait_send()
        for d in range(sides):
            core_copy(d, g).wait_send()

    def drain(step):
        for direction, piece in every:
            hop(direction, step, piece).wait_send()

    if half > 1:
        drain(0)
    loop(1, half - 1, drain)
    for direction, piece in moves(True):
        hop(direction, half - 1, piece).wait_send()


def per_device(left_factor, right_factor, block_columns, labels):
    count, layers = lax.axis_size("row"), lax.axis_size("layer")
    size, width = right_factor.shape
    rows = left_factor.shape[0]
    trows = labels.shape[0]
    part, half, sides = width // layers, count // 2, layers // 2
    dma = pltpu.SemaphoreType.DMA
    return pl.pallas_call(
        functools.partial(kernel, count, layers),
        out_shape=pltpu.VMEM((rows, part), F32),
        in_specs=[
            pl.BlockSpec(memory_space=pl.ANY),
            pl.BlockSpec(memory_space=pl.ANY),
            pl.BlockSpec(memory_space=pl.ANY),
            pl.BlockSpec(memory_space=pl.ANY),
        ],
        out_specs=pl.BlockSpec(memory_space=pltpu.VMEM),
        scratch_shapes=[
            pltpu.VMEM((count, size, width), F32),
            pltpu.VMEM((rows, width), F32),
            pltpu.VMEM((rows, width), BF16),
            pltpu.VMEM((rows, width), BF16),
            pltpu.VMEM(labels.shape, jnp.int32),
            pltpu.SMEM(block_columns.shape[::-1], jnp.int32),
            pltpu.VMEM((layers, rows, part), F32),
            pltpu.VMEM((sides, rows, part), F32),
            pltpu.VMEM((max(sides - 1, 1), rows, part), F32),
            pltpu.VMEM((max(sides - 1, 1), rows, part), F32),
            dma((4,)),
            dma((2, half, pieces)),
            dma((2, half, pieces)),
            dma((sides, trows)),
            dma((sides, trows)),
            dma((max(sides - 1, 1), trows)),
            dma((max(sides - 1, 1), trows)),
        ],
        compiler_params=pltpu.CompilerParams(
            collective_id=0, has_side_effects=True, vmem_limit_bytes=56 * 1024 * 1024
        ),
        cost_estimate=pl.CostEstimate(
            flops=12 * rows * width * size * count,
            bytes_accessed=4 * (rows * width + count * size * width + labels.size + rows * part),
            transcendentals=rows * size * count,
        ),
    )(left_factor, right_factor, block_columns.T, labels)


def solution(mesh):
    in_specs = (
        P("row", None),
        P(("row", "layer"), None),
        P("row", "layer"),
        P("row", "layer", None, None),
    )
    out_specs = P("row", "layer")
    return jax.shard_map(
        per_device, mesh=mesh, in_specs=in_specs, out_specs=out_specs, check_vma=False
    )
```
